512 devices in a mesh: row: 64 (over z_hi, y, core), col: 8 (over x, z_lo).
Axes of the slice: x: 4, y: 8, z: 8 (z_hi: 4, z_lo: 2; z = z_hi * 2 + z_lo), core: 2. Of those that a mesh axis runs over, the one named last changes fastest.
Arguments:
- counts: int32 [49152, 9216], P('row', 'col'), may hold values from 0 to 63
- row_marg: int32 [49152], P('row'), may hold values from 1 to 24570
- col_marg: int32 [9216], P('col'), may hold values from 49152 to 3096576
- row_emb: float32 [300, 49152], P(None, ('row', 'col')), may hold values from -0.375 to 0.375
- col_emb: float32 [300, 9216], P(None, ('col', 'row')), may hold values from -0.375 to 0.375
- row_acc: float32 [300, 49152], P(None, ('row', 'col')), may hold values from 10 to 1000
- col_acc: float32 [300, 9216], P(None, ('col', 'row')), may hold values from 10 to 1000
Outputs:
- new_row_emb: float32 [300, 49152], P(None, ('row', 'col'))
- new_col_emb: float32 [300, 9216], P(None, ('col', 'row'))
- new_row_acc: float32 [300, 49152], P(None, ('row', 'col'))
- new_col_acc: float32 [300, 9216], P(None, ('col', 'row'))
The draws below stay inside these ranges and needn't reach their ends.
All inputs are finite; a program needn't handle non-finite values.
Results may differ from the reference program's by a relative error of at most 0.0078.
Values may be sent and summed in bfloat16 or wider, within the bound.
No kernel may reach another device: no remote copies, remote signals or barrier semaphores. Data moves between devices by JAX's collectives and lax.ppermute only.
A program may use at most 64 MiB of HBM per device.

```python
import math
import jax
import jax.numpy as jnp
from jax import lax

D = 300
BR = 768
ROWS = 49152
COLS = 9216
N_ROW = 64


def draw_counts(key, part):
    key = jax.random.fold_in(key, 11)
    key_level, key_extra, key_vacant = jax.random.split(key, 3)
    shape = (ROWS, COLS)
    exponent = jax.random.randint(key_level, shape, 0, 6)
    lowest = jnp.left_shift(jnp.ones(shape, jnp.int32), exponent)
    surplus = jax.random.randint(key_extra, shape, 0, lowest)
    vacant = jax.random.randint(key_vacant, shape, 0, 5) < 2
    return jnp.where(vacant, 0, lowest + surplus).astype(jnp.int32)


def spread_draw(key, total, levels):
    key_level, key_extra = jax.random.split(key)
    places = jnp.arange(total, dtype=jnp.int32)
    exponent = jax.random.randint(key_level, (total,), 0, levels)
    exponent = jnp.where(places == 0, levels - 1, exponent)
    exponent = jnp.where(places == total - 1, 0, exponent)
    lowest = jnp.left_shift(jnp.ones((total,), jnp.int32), exponent)
    surplus = jax.random.randint(key_extra, (total,), 0, lowest)
    surplus = jnp.where(places == 0, lowest - 1, surplus)
    return (places, lowest + surplus)


def draw_row_marg(key, part):
    key = jax.random.fold_in(key, 23)
    places, values = spread_draw(key, ROWS, 12)
    factor = 1 + 6 * (ROWS - 1 - places) // ROWS
    return (values * factor).astype(jnp.int32)


def draw_col_marg(key, part):
    key = jax.random.fold_in(key, 37)
    places, values = spread_draw(key, COLS, 6)
    return (values * ROWS).astype(jnp.int32)


def block_levels(key, shape, pieces, low, largest):
    def one(axis_at, blocks):
        heights = jax.random.uniform(jax.random.fold_in(jax.random.fold_in(key, 6), axis_at), (blocks,), jnp.float32, low / len(pieces), largest / len(pieces))
        return jnp.repeat(jnp.exp(heights), shape[axis_at] // blocks).reshape((-1,) + (1,) * (len(shape) - axis_at - 1))

    gain = one(*pieces[0])
    for cut in pieces[1:]:
        gain = gain * one(*cut)
    return gain


def normal_values(rng, extent, scale, bound, shards=(), kind=jnp.bfloat16):
    entries = scale * jax.random.normal(rng, extent, jnp.float32)
    if shards:
        entries = entries * block_levels(rng, extent, shards, -0.22, 0.18)
    return jnp.clip(entries, -bound, bound).astype(kind)


def setup_inputs(seed: int = 0) -> dict:
    splits = jax.random.split(jax.random.key(seed), 8)
    return {
        "counts": draw_counts(jax.random.fold_in(splits[7], 71), 0),
        "row_marg": draw_row_marg(jax.random.fold_in(splits[7], 71), 0),
        "col_marg": draw_col_marg(jax.random.fold_in(splits[7], 71), 0),
        "row_emb": normal_values(splits[3], (D, ROWS), D ** -0.5, 0.375, ((1, 512),), jnp.float32),
        "col_emb": normal_values(splits[4], (D, COLS), D ** -0.5, 0.375, ((1, 512),), jnp.float32),
        "row_acc": jnp.clip(jnp.exp(math.log(1000.0) - 4.6051702 * jax.random.uniform(splits[5], (D, ROWS), jnp.float32) ** block_levels(splits[5], (D, ROWS), ((1, 512),), -0.2, 0.2)), 10.0, 1000.0),
        "col_acc": jnp.clip(jnp.exp(math.log(1000.0) - 4.6051702 * jax.random.uniform(splits[6], (D, COLS), jnp.float32) ** block_levels(splits[6], (D, COLS), ((1, 512),), -0.2, 0.2)), 10.0, 1000.0),
    }


def cell_gradient(counts, row_log, col_log, log_total, scores):
    pmi_base = log_total - row_log[:, None] - col_log[None, :]
    count_float = counts.astype(jnp.float32)
    weight = 0.1 + 0.25 * jnp.sqrt(count_float)
    fitted = weight * (scores - pmi_base - jnp.log(jnp.maximum(count_float, 1.0)))
    return jnp.where(counts > 0, fitted, jax.nn.sigmoid(scores - pmi_base)).astype(jnp.bfloat16)

def adagrad(embedding, accumulator, gradient):
    new_acc = accumulator + gradient * gradient
    return (embedding - gradient / jnp.sqrt(new_acc), new_acc)

def reference(counts, row_marg, col_marg, row_emb, col_emb, row_acc, col_acc):
    log_total = jnp.log(jnp.sum(row_marg.astype(jnp.float32)))
    row_half = row_emb.astype(jnp.bfloat16)
    col_half = col_emb.astype(jnp.bfloat16)
    row_log_all = jnp.log(row_marg.astype(jnp.float32))
    col_log = jnp.log(col_marg.astype(jnp.float32))

    def block(col_total, block_index):
        start = (block_index * BR).astype(jnp.int32)
        count_rows = lax.dynamic_slice_in_dim(counts, start, BR, 0)
        row_log = lax.dynamic_slice_in_dim(row_log_all, start, BR, 0)
        rows_half = lax.dynamic_slice_in_dim(row_half, start, BR, 1)
        scores = lax.dot_general(rows_half, col_half, (((0,), (0,)), ((), ())), preferred_element_type=jnp.float32)
        cell_slope = cell_gradient(count_rows, row_log, col_log, log_total, scores)
        row_part = lax.dot_general(col_half, cell_slope, (((1,), (1,)), ((), ())), preferred_element_type=jnp.float32)
        col_part = lax.dot_general(rows_half, cell_slope, (((1,), (0,)), ((), ())), preferred_element_type=jnp.float32)
        return (col_total + col_part, row_part)
    col_grad, row_parts = lax.scan(block, jnp.zeros((D, COLS), jnp.float32), jnp.arange(N_ROW, dtype=jnp.int32))
    row_grad = jnp.transpose(row_parts, (1, 0, 2)).reshape(D, ROWS)
    new_row_emb, new_row_acc = adagrad(row_emb, row_acc, row_grad)
    new_col_emb, new_col_acc = adagrad(col_emb, col_acc, col_grad)
    return (new_row_emb, new_col_emb, new_row_acc, new_col_acc)
```

```python
import jax
import jax.numpy as jnp
from jax import lax
from jax.sharding import Mesh, PartitionSpec as P

ROW_AXES = ("zh", "y", "core")
COL_AXES = ("x", "zl")
CHIP_AXES = ("zh", "y")


def cell_gradient(counts, row_log, col_log, log_total, scores):
    pmi_base = log_total - row_log[:, None] - col_log[None, :]
    count_float = counts.astype(jnp.float32)
    weight = 0.1 + 0.25 * jnp.sqrt(count_float)
    fitted = weight * (scores - pmi_base - jnp.log(jnp.maximum(count_float, 1.0)))
    return jnp.where(counts > 0, fitted, jax.nn.sigmoid(scores - pmi_base)).astype(jnp.bfloat16)


def adagrad(embedding, accumulator, gradient):
    new_acc = accumulator + gradient * gradient
    return (embedding - gradient / jnp.sqrt(new_acc), new_acc)


def split3(value):
    high = lax.reduce_precision(value, 8, 7)
    middle = lax.reduce_precision(value - high, 8, 7)
    low = lax.reduce_precision(value - high - middle, 8, 7)
    return jnp.stack([high, middle, low]).astype(jnp.bfloat16)


def exchange(blocks, axes):
    return lax.all_to_all(blocks, axes, 0, 0, tiled=True)


def swap(block):
    return lax.ppermute(block, "core", [(0, 1), (1, 0)])


def body(counts, row_marg, col_marg, row_emb, col_emb, row_acc, col_acc):
    n_col = lax.axis_size(COL_AXES)
    n_chip = lax.axis_size(CHIP_AXES)
    core = lax.axis_index("core")
    rows, cols = counts.shape
    depth, own_cols = col_emb.shape

    row_own = row_emb.T.astype(jnp.bfloat16)
    col_own = col_emb.T.astype(jnp.bfloat16)
    local_total = jnp.sum(row_marg).astype(jnp.float32)
    extra = jnp.zeros((1, depth), jnp.bfloat16).at[0, :3].set(split3(local_total))
    packed = jnp.concatenate([col_own, extra], axis=0)

    mine = exchange(jnp.broadcast_to(packed[None], (n_chip,) + packed.shape), CHIP_AXES)
    row_half = exchange(jnp.broadcast_to(row_own[None], (n_col,) + row_own.shape), COL_AXES)
    row_half = row_half.reshape(rows, depth)
    other = swap(mine)
    first = jnp.where(core == 0, mine, other)
    second = jnp.where(core == 0, other, mine)
    both = jnp.stack([first, second], axis=1)
    col_half = both[:, :, :own_cols].reshape(cols, depth)
    log_total = jnp.log(jnp.sum(both[:, :, own_cols, :3].astype(jnp.float32)))

    scores = lax.dot_general(
        row_half, col_half, (((1,), (1,)), ((), ())), preferred_element_type=jnp.float32
    )
    row_log = jnp.log(row_marg.astype(jnp.float32))
    col_log = jnp.log(col_marg.astype(jnp.float32))
    cell_slope = cell_gradient(counts, row_log, col_log, log_total, scores)
    col_grad = lax.dot_general(
        cell_slope, row_half, (((0,), (0,)), ((), ())), preferred_element_type=jnp.float32
    )
    row_grad = lax.dot_general(
        cell_slope, col_half, (((1,), (0,)), ((), ())), preferred_element_type=jnp.float32
    )

    col_parts = col_grad.astype(jnp.bfloat16).reshape(n_chip, 2, own_cols, depth)
    keep = jnp.where(core == 0, col_parts[:, 0], col_parts[:, 1])
    give = jnp.where(core == 0, col_parts[:, 1], col_parts[:, 0])
    pair = (keep.astype(jnp.float32) + swap(give).astype(jnp.float32)).astype(jnp.bfloat16)
    col_share = jnp.sum(exchange(pair, CHIP_AXES).astype(jnp.float32), axis=0)
    row_parts = row_grad.astype(jnp.bfloat16).reshape(n_col, rows // n_col, depth)
    row_share = jnp.sum(exchange(row_parts, COL_AXES).astype(jnp.float32), axis=0)

    new_row_emb, new_row_acc = adagrad(row_emb.T, row_acc.T, row_share)
    new_col_emb, new_col_acc = adagrad(col_emb.T, col_acc.T, col_share)
    return (new_row_emb.T, new_col_emb.T, new_row_acc.T, new_col_acc.T)


def solution(mesh):
    fine = Mesh(mesh.devices.reshape(4, 8, 2, 4, 2), ("zh", "y", "core", "x", "zl"))
    return jax.shard_map(
        body,
        mesh=fine,
        in_specs=(
            P(ROW_AXES, COL_AXES),
            P(ROW_AXES),
            P(COL_AXES),
            P(None, ROW_AXES + COL_AXES),
            P(None, COL_AXES + ROW_AXES),
            P(None, ROW_AXES + COL_AXES),
            P(None, COL_AXES + ROW_AXES),
        ),
        out_specs=(
            P(None, ROW_AXES + COL_AXES),
            P(None, COL_AXES + ROW_AXES),
            P(None, ROW_AXES + COL_AXES),
            P(None, COL_AXES + ROW_AXES),
        ),
        check_vma=False,
    )
```

```python
import functools

import jax
import jax.numpy as jnp
from jax import lax
from jax.experimental import pallas as pl
from jax.experimental.pallas import tpu as pltpu
from jax.sharding import Mesh, PartitionSpec as P

ROW_AXES = ("zh", "y", "core")
COL_AXES = ("x", "zl")
CHIP_AXES = ("zh", "y")
GROUP = 24
WINDOW = 640
WIDE = 384
F32, BF16 = jnp.float32, jnp.bfloat16
PARAMS = pltpu.CompilerParams(vmem_limit_bytes=20 * 1024 * 1024)


def widen(value):
    rows, depth = value.shape
    return jnp.concatenate([value, jnp.zeros((rows, WIDE - depth), value.dtype)], axis=1)


def prep_kernel(marg_hbm, col_hbm, row_hbm, send_ref, own_ref, marg, block, rows, sems):
    words = col_hbm.shape[0]
    load_marg = pltpu.make_async_copy(marg_hbm, marg, sems.at[0])
    load_col = pltpu.make_async_copy(col_hbm, block, sems.at[1])
    load_row = pltpu.make_async_copy(row_hbm, rows, sems.at[2])
    load_marg.start()
    load_col.start()
    load_row.start()
    load_marg.wait()
    total = jnp.sum(marg[...], axis=(0, 1), keepdims=True).astype(F32)
    high = total.astype(BF16).astype(F32)
    middle = (total - high).astype(BF16).astype(F32)
    low = total - high - middle
    line = lax.broadcasted_iota(jnp.int32, (GROUP - words, WIDE), 0)
    lane = lax.broadcasted_iota(jnp.int32, (GROUP - words, WIDE), 1)
    parts = jnp.where(lane == 0, high, jnp.where(lane == 1, middle, jnp.where(lane == 2, low, 0.0)))
    load_col.wait()
    value = jnp.concatenate([widen(block[...]), jnp.where(line == 0, parts, 0.0)], axis=0).astype(BF16)
    for i in range(send_ref.shape[0]):
        send_ref[i] = value
    load_row.wait()
    own_ref[...] = widen(rows[...]).astype(BF16)


def prepare(row_marg, col_t, row_t, n_chip):
    return pl.pallas_call(
        prep_kernel,
        in_specs=[pl.BlockSpec(memory_space=pltpu.HBM)] * 3,
        out_shape=(
            jax.ShapeDtypeStruct((n_chip, GROUP, WIDE), BF16),
            jax.ShapeDtypeStruct((row_t.shape[0], WIDE), BF16),
        ),
        scratch_shapes=[
            pltpu.VMEM(row_marg.shape, jnp.int32),
            pltpu.VMEM(col_t.shape, F32),
            pltpu.VMEM(row_t.shape, F32),
            pltpu.SemaphoreType.DMA((3,)),
        ],
        compiler_params=PARAMS,
    )(*[pltpu.with_memory_space_constraint(a, pltpu.HBM) for a in (row_marg, col_t, row_t)])


def group_of(number):
    return jnp.right_shift(number * 2731, 16)


def cells_kernel(words, marg_ref, counts_hbm, count_ref, logs_ref, counts, pick, sems):
    rows, cols = counts_hbm.shape
    cells = count_ref.shape[0] // 2
    half = cells // 2
    block = 256
    loads = [
        pltpu.make_async_copy(counts_hbm.at[r : r + block], counts.at[r : r + block], sems.at[r // block])
        for r in range(0, rows, block)
    ]
    for load in loads:
        load.start()
    log = jnp.log(marg_ref[...].astype(F32))
    high = log.astype(BF16).astype(F32)
    middle = (log - high).astype(BF16).astype(F32)
    low = log - high - middle
    line = lax.broadcasted_iota(jnp.int32, (128, cols), 0)
    stack = jnp.where(line == 0, high, jnp.where(line == 1, middle, jnp.where(line == 2, low, 1.0)))
    stack = stack.astype(BF16)
    lane = lax.broadcasted_iota(jnp.int32, (half, WINDOW), 1)
    place = lax.broadcasted_iota(jnp.int32, (half, 1), 0)
    group = group_of(place)
    word = place - GROUP * group
    column = lax.broadcasted_iota(jnp.int32, (half, 128), 1)
    for m in range(2):
        window = slice(m * (cols - WINDOW), m * (cols - WINDOW) + WINDOW)
        for c in range(2):
            target = (2 * group + (m * half // GROUP * 2 + c)) * words + word - window.start
            target = jnp.where(word < words, target, -1)
            at = slice(c * cells + m * half, c * cells + (m + 1) * half)
            hit = jnp.where(lane == target, 1.0, 0.0).astype(BF16)
            pick[at, :] = hit
            found = lax.dot_general(hit, stack[:, window], (((1,), (1,)), ((), ())), preferred_element_type=F32)
            found = jnp.where(column < 3, found, 0.0)
            found = jnp.where((column == 0) & (word >= words), -1e30, found)
            logs_ref[at, :] = found.astype(BF16)
    for r in range(0, rows, block):
        loads[r // block].wait()
        for m in range(2):
            window = slice(m * (cols - WINDOW), m * (cols - WINDOW) + WINDOW)
            part = counts[r : r + block, window].astype(F32).astype(BF16)
            for c in range(2):
                at = slice(c * cells + m * half, c * cells + (m + 1) * half)
                count = lax.dot_general(pick[at, :], part, (((1,), (1,)), ((), ())), preferred_element_type=F32)
                count_ref[at, r : r + block] = count.astype(jnp.int32).astype(jnp.int8)


def cell_tables(counts, col_marg, n_chip, words):
    rows, cols = counts.shape
    cells = n_chip * GROUP
    return pl.pallas_call(
        functools.partial(cells_kernel, words),
        in_specs=[pl.BlockSpec(memory_space=pltpu.VMEM), pl.BlockSpec(memory_space=pltpu.HBM)],
        out_shape=(jax.ShapeDtypeStruct((2 * cells, rows), jnp.int8), jax.ShapeDtypeStruct((2 * cells, 128), BF16)),
        scratch_shapes=[
            pltpu.VMEM((rows, cols), jnp.int32),
            pltpu.VMEM((2 * cells, WINDOW), BF16),
            pltpu.SemaphoreType.DMA((rows // 256,)),
        ],
        compiler_params=PARAMS,
    )(col_marg, pltpu.with_memory_space_constraint(counts, pltpu.HBM))


def rows_kernel(place_ref, mine_ref, other_ref, out_ref):
    x, zl = place_ref[0], place_ref[1]
    for i in range(4):
        block = 2 * jnp.bitwise_xor(x, i) + zl
        out_ref[block] = mine_ref[i]
        out_ref[jnp.bitwise_xor(block, 1)] = other_ref[i]


def assemble_rows(place, mine, other):
    n, size, depth = mine.shape
    return pl.pallas_call(
        rows_kernel,
        grid_spec=pltpu.PrefetchScalarGridSpec(
            num_scalar_prefetch=1,
            grid=(1,),
            in_specs=[pl.BlockSpec((n, size, depth), lambda i, s: (0, 0, 0))] * 2,
            out_specs=pl.BlockSpec((2 * n, size, depth), lambda i, s: (0, 0, 0)),
        ),
        out_shape=jax.ShapeDtypeStruct((2 * n, size, depth), BF16),
        compiler_params=PARAMS,
    )(place, mine, other)


def slope_kernel(words, half_ref, col_ref, rest_ref, row_ref, marg_ref, count_ref, logs_ref, slope_ref, grad_ref):
    cells, rows = slope_ref.shape
    place = lax.broadcasted_iota(jnp.int32, (16, cells), 1)
    pick = jnp.where(place - GROUP * group_of(place) == words, 1.0, 0.0).astype(BF16)
    parts = jnp.dot(pick, col_ref[...], preferred_element_type=F32)
    parts += jnp.dot(pick, rest_ref[...], preferred_element_type=F32)
    log_total = jnp.log(jnp.sum(parts[0:1, 0:128], axis=1, keepdims=True))
    row_base = jnp.log(marg_ref[...].astype(F32)) - log_total
    first = half_ref[0] * cells
    row_half = row_ref[...]
    block = 256
    for b in range(0, cells, block):
        at = pl.ds(pl.multiple_of(first + b, block), block)
        score = lax.dot_general(
            col_ref[b : b + block, :], row_half, (((1,), (1,)), ((), ())), preferred_element_type=F32
        )
        count = count_ref[at, :].astype(jnp.int32).astype(F32)
        logs = logs_ref[at, :].astype(F32)
        excess = score + (row_base + (logs[:, 0:1] + logs[:, 1:2] + logs[:, 2:3]))
        fitted = (0.1 + 0.25 * jnp.sqrt(count)) * (excess - jnp.log(jnp.maximum(count, 1.0)))
        slope = jnp.where(count > 0.0, fitted, 0.5 + 0.5 * jnp.tanh(0.5 * excess)).astype(BF16)
        slope_ref[b : b + block, :] = slope
        grad = jnp.dot(slope, row_half, preferred_element_type=F32)
        grad_ref[b : b + block, :] = grad.astype(grad_ref.dtype)


def slopes(half, col_half, col_rest, row_half, row_marg, count, logs, words, kind):
    cells, rows = col_half.shape[0], row_half.shape[0]
    vmem = pl.BlockSpec(memory_space=pltpu.VMEM)
    return pl.pallas_call(
        functools.partial(slope_kernel, words),
        in_specs=[pl.BlockSpec(memory_space=pltpu.SMEM)] + [vmem] * 6,
        out_shape=[jax.ShapeDtypeStruct((cells, rows), BF16), jax.ShapeDtypeStruct((cells, WIDE), kind)],
        compiler_params=PARAMS,
    )(half, col_half, col_rest, row_half, row_marg, count, logs)


def row_grad_kernel(place_ref, own_ref, other_ref, keep_slope_ref, give_slope_ref, keep_ref, give_ref, total):
    x, zl = place_ref[0], place_ref[1]
    size = keep_ref.shape[1]
    contract = (((0,), (0,)), ((), ()))
    grad = lax.dot_general(own_ref[...], keep_slope_ref[...], contract, preferred_element_type=F32)
    grad += lax.dot_general(other_ref[...], give_slope_ref[...], contract, preferred_element_type=F32)
    total[...] = grad.T
    for i in range(4):
        block = 2 * jnp.bitwise_xor(x, i) + zl
        keep_ref[i] = total[pl.ds(pl.multiple_of(block * size, size), size), :]
        block = jnp.bitwise_xor(block, 1)
        give_ref[i] = total[pl.ds(pl.multiple_of(block * size, size), size), :].astype(BF16)


def row_grads(place, own, other, keep_slope, give_slope, size):
    rows = keep_slope.shape[1]
    vmem = pl.BlockSpec(memory_space=pltpu.VMEM)
    return pl.pallas_call(
        row_grad_kernel,
        in_specs=[pl.BlockSpec(memory_space=pltpu.SMEM)] + [vmem] * 4,
        out_shape=[
            jax.ShapeDtypeStruct((4, size, WIDE), F32),
            jax.ShapeDtypeStruct((4, size, WIDE), BF16),
        ],
        scratch_shapes=[pltpu.VMEM((rows, WIDE), F32)],
        compiler_params=PARAMS,
    )(place, own, other, keep_slope, give_slope)


def after(value, *others):
    anywhere = pl.BlockSpec(memory_space=pl.ANY)
    return pl.pallas_call(
        lambda *refs: None,
        in_specs=[anywhere] * (1 + len(others)),
        out_specs=anywhere,
        out_shape=jax.ShapeDtypeStruct(value.shape, value.dtype),
        input_output_aliases={0: 0},
        compiler_params=pltpu.CompilerParams(vmem_limit_bytes=1024 * 1024),
    )(value, *others)


def adagrad(embedding, accumulator, gradient):
    new_acc = accumulator + gradient * gradient
    return (embedding - gradient / jnp.sqrt(new_acc), new_acc)


def exchange(blocks):
    return lax.all_to_all(blocks, CHIP_AXES, 0, 0, tiled=True)


def flip(block, axis, mask):
    return lax.ppermute(block, axis, [(i, i ^ mask) for i in range(lax.axis_size(axis))])


def body(counts, row_marg, col_marg, row_emb, col_emb, row_acc, col_acc):
    n_chip = lax.axis_size(CHIP_AXES)
    rows, cols = counts.shape
    depth, words = col_emb.shape
    size = row_emb.shape[1]
    core = lax.axis_index("core")
    place = jnp.stack([lax.axis_index("x"), lax.axis_index("zl"), core]).astype(jnp.int32)

    row_line, col_line = row_marg.reshape(1, rows), col_marg.reshape(1, cols)
    send, own = prepare(row_marg.reshape(rows // 128, 128), col_emb.T, row_emb.T, n_chip)
    mine = exchange(send)
    stack = jnp.stack([own] + [flip(own, "x", k) for k in (1, 2, 3)])
    row_half = assemble_rows(place, stack, flip(stack, "zl", 1)).reshape(rows, WIDE)
    count, logs = cell_tables(counts, col_line, n_chip, words)
    shape = (n_chip, GROUP, WIDE)
    mine = after(mine, row_half, count)
    far = flip(mine, "core", 1).reshape(n_chip * GROUP, WIDE)
    near = mine.reshape(n_chip * GROUP, WIDE)

    give_slope, give = slopes((1 - core).reshape(1), far, near, row_half, row_line, count, logs, words, BF16)
    other = flip(give.reshape(shape), "core", 1)
    keep_slope, keep = slopes(core.reshape(1), near, far, row_half, row_line, count, logs, words, F32)
    pair = (keep.reshape(shape) + other.astype(F32)).astype(BF16)
    col_share = jnp.sum(exchange(pair)[:, :words, :depth].astype(F32), axis=0)

    row_keep, row_give = row_grads(place, near, far, keep_slope, give_slope, size)
    row_keep = row_keep + flip(row_give, "zl", 1).astype(F32)
    row_share = row_keep[0]
    for k in (1, 2, 3):
        row_share = row_share + flip(row_keep[k].astype(BF16), "x", k).astype(F32)
    row_share = row_share[:, :depth]

    new_row_emb, new_row_acc = adagrad(row_emb.T, row_acc.T, row_share)
    new_col_emb, new_col_acc = adagrad(col_emb.T, col_acc.T, col_share)
    return (new_row_emb.T, new_col_emb.T, new_row_acc.T, new_col_acc.T)


def solution(mesh):
    fine = Mesh(mesh.devices.reshape(4, 8, 2, 4, 2), ("zh", "y", "core", "x", "zl"))
    return jax.shard_map(
        body,
        mesh=fine,
        in_specs=(
            P(ROW_AXES, COL_AXES),
            P(ROW_AXES),
            P(COL_AXES),
            P(None, ROW_AXES + COL_AXES),
            P(None, COL_AXES + ROW_AXES),
            P(None, ROW_AXES + COL_AXES),
            P(None, COL_AXES + ROW_AXES),
        ),
        out_specs=(
            P(None, ROW_AXES + COL_AXES),
            P(None, COL_AXES + ROW_AXES),
            P(None, ROW_AXES + COL_AXES),
            P(None, COL_AXES + ROW_AXES),
        ),
        check_vma=False,
    )
```

```python
import functools

import jax
import jax.numpy as jnp
from jax import lax
from jax.experimental import pallas as pl
from jax.experimental.pallas import tpu as pltpu
from jax.sharding import Mesh, PartitionSpec as P

ROW_AXES = ("zh", "y", "core")
COL_AXES = ("x", "zl")
CHIP_AXES = ("zh", "y")
GROUP = 24
WINDOW = 640
WIDE = 384
F32, BF16 = jnp.float32, jnp.bfloat16
PARAMS = pltpu.CompilerParams(vmem_limit_bytes=20 * 1024 * 1024)


def widen(value):
    rows, depth = value.shape
    return jnp.concatenate([value, jnp.zeros((rows, WIDE - depth), value.dtype)], axis=1)


def own_kernel(marg_hbm, row_hbm, col_hbm, own_ref, col_ref, total_ref, marg, rows, cols, sems):
    load_marg = pltpu.make_async_copy(marg_hbm, marg, sems.at[0])
    load_row = pltpu.make_async_copy(row_hbm, rows, sems.at[1])
    load_col = pltpu.make_async_copy(col_hbm, cols, sems.at[2])
    load_marg.start()
    load_row.start()
    load_col.start()
    load_marg.wait()
    total = jnp.sum(marg[...], axis=(0, 1), keepdims=True).astype(F32)
    total_ref[...] = jnp.broadcast_to(total, total_ref.shape)
    load_row.wait()
    own_ref[...] = widen(rows[...]).astype(BF16)
    load_col.wait()
    rest = GROUP - cols.shape[0]
    col_ref[...] = jnp.concatenate([widen(cols[...]), jnp.zeros((rest, WIDE), F32)], axis=0)


def prepare_own(row_marg, row_t, col_t):
    return pl.pallas_call(
        own_kernel,
        in_specs=[pl.BlockSpec(memory_space=pltpu.HBM)] * 3,
        out_shape=(
            jax.ShapeDtypeStruct((row_t.shape[0], WIDE), BF16),
            jax.ShapeDtypeStruct((GROUP, WIDE), F32),
            jax.ShapeDtypeStruct((8, 128), F32),
        ),
        scratch_shapes=[
            pltpu.VMEM(row_marg.shape, jnp.int32),
            pltpu.VMEM(row_t.shape, F32),
            pltpu.VMEM(col_t.shape, F32),
            pltpu.SemaphoreType.DMA((3,)),
        ],
        compiler_params=PARAMS,
    )(*[pltpu.with_memory_space_constraint(a, pltpu.HBM) for a in (row_marg, row_t, col_t)])


def send_kernel(words, total_ref, rest_ref, col_ref, send_ref):
    total = total_ref[0:1, 0:1] + rest_ref[0:1, 0:1]
    high = total.astype(BF16).astype(F32)
    middle = (total - high).astype(BF16).astype(F32)
    low = total - high - middle
    line = lax.broadcasted_iota(jnp.int32, (GROUP, WIDE), 0)
    lane = lax.broadcasted_iota(jnp.int32, (GROUP, WIDE), 1)
    parts = jnp.where(lane == 0, high, jnp.where(lane == 1, middle, jnp.where(lane == 2, low, 0.0)))
    value = jnp.where(line == words, parts, col_ref[...]).astype(BF16)
    for i in range(send_ref.shape[0]):
        send_ref[i] = value


def prepare_send(total, rest, col_own, n_chip, words):
    return pl.pallas_call(
        functools.partial(send_kernel, words),
        out_shape=jax.ShapeDtypeStruct((n_chip, GROUP, WIDE), BF16),
        compiler_params=PARAMS,
    )(total, rest, col_own)


def group_of(number):
    return jnp.right_shift(number * 2731, 16)


def cells_kernel(words, marg_ref, counts_hbm, count_ref, logs_ref, counts, pick, sems):
    rows, cols = counts_hbm.shape
    cells = count_ref.shape[0] // 2
    half = cells // 2
    block = 256
    loads = [
        pltpu.make_async_copy(counts_hbm.at[r : r + block], counts.at[r : r + block], sems.at[r // block])
        for r in range(0, rows, block)
    ]
    for load in loads:
        load.start()
    log = jnp.log(marg_ref[...].astype(F32))
    high = log.astype(BF16).astype(F32)
    middle = (log - high).astype(BF16).astype(F32)
    low = log - high - middle
    line = lax.broadcasted_iota(jnp.int32, (128, cols), 0)
    stack = jnp.where(line == 0, high, jnp.where(line == 1, middle, jnp.where(line == 2, low, 1.0)))
    stack = stack.astype(BF16)
    lane = lax.broadcasted_iota(jnp.int32, (half, WINDOW), 1)
    place = lax.broadcasted_iota(jnp.int32, (half, 1), 0)
    group = group_of(place)
    word = place - GROUP * group
    column = lax.broadcasted_iota(jnp.int32, (half, 128), 1)
    for m in range(2):
        window = slice(m * (cols - WINDOW), m * (cols - WINDOW) + WINDOW)
        for c in range(2):
            target = (2 * group + (m * half // GROUP * 2 + c)) * words + word - window.start
            target = jnp.where(word < words, target, -1)
            at = slice(c * cells + m * half, c * cells + (m + 1) * half)
            hit = jnp.where(lane == target, 1.0, 0.0).astype(BF16)
            pick[at, :] = hit
            found = lax.dot_general(hit, stack[:, window], (((1,), (1,)), ((), ())), preferred_element_type=F32)
            found = jnp.where(column < 3, found, 0.0)
            found = jnp.where((column == 0) & (word >= words), -1e30, found)
            logs_ref[at, :] = found.astype(BF16)
    for r in range(0, rows, block):
        loads[r // block].wait()
        for m in range(2):
            window = slice(m * (cols - WINDOW), m * (cols - WINDOW) + WINDOW)
            part = counts[r : r + block, window].astype(F32).astype(BF16)
            for c in range(2):
                at = slice(c * cells + m * half, c * cells + (m + 1) * half)
                count = lax.dot_general(pick[at, :], part, (((1,), (1,)), ((), ())), preferred_element_type=F32)
                count_ref[at, r : r + block] = count.astype(jnp.int32).astype(jnp.int8)


def cell_tables(counts, col_marg, n_chip, words):
    rows, cols = counts.shape
    cells = n_chip * GROUP
    return pl.pallas_call(
        functools.partial(cells_kernel, words),
        in_specs=[pl.BlockSpec(memory_space=pltpu.VMEM), pl.BlockSpec(memory_space=pltpu.HBM)],
        out_shape=(jax.ShapeDtypeStruct((2 * cells, rows), jnp.int8), jax.ShapeDtypeStruct((2 * cells, 128), BF16)),
        scratch_shapes=[
            pltpu.VMEM((rows, cols), jnp.int32),
            pltpu.VMEM((2 * cells, WINDOW), BF16),
            pltpu.SemaphoreType.DMA((rows // 256,)),
        ],
        compiler_params=PARAMS,
    )(col_marg, pltpu.with_memory_space_constraint(counts, pltpu.HBM))


def rows_kernel(place_ref, *refs):
    x, zl = place_ref[0], place_ref[1]
    for k in range(4):
        for b in range(2):
            block = 2 * jnp.bitwise_xor(x, k) + jnp.bitwise_xor(zl, b)
            refs[4][block] = refs[k][b]


def assemble_rows(place, pairs):
    size, depth = pairs[0].shape[1:]
    vmem = pl.BlockSpec(memory_space=pltpu.VMEM)
    return pl.pallas_call(
        rows_kernel,
        in_specs=[pl.BlockSpec(memory_space=pltpu.SMEM)] + [vmem] * 4,
        out_shape=jax.ShapeDtypeStruct((8, size, depth), BF16),
        compiler_params=PARAMS,
    )(place, *pairs)


def slope_kernel(words, half_ref, order_ref, col_ref, near_ref, row_ref, marg_ref, count_ref, logs_ref, slope_ref, grad_ref):
    cells, rows = slope_ref.shape
    place = lax.broadcasted_iota(jnp.int32, (16, cells), 1)
    pick = jnp.where(place - GROUP * group_of(place) == words, 1.0, 0.0).astype(BF16)
    parts = jnp.dot(pick, near_ref[...], preferred_element_type=F32)
    log_total = jnp.log(jnp.sum(parts[0:1, 0:128], axis=1, keepdims=True))
    row_base = jnp.log(marg_ref[...].astype(F32)) - log_total
    first = half_ref[0] * cells
    row_half = row_ref[...]
    block = 256
    for b in range(0, cells, block):
        at = pl.ds(pl.multiple_of(first + b, block), block)
        score = lax.dot_general(
            col_ref[b : b + block, :], row_half, (((1,), (1,)), ((), ())), preferred_element_type=F32
        )
        count = count_ref[at, :].astype(jnp.int32).astype(F32)
        logs = logs_ref[at, :].astype(F32)
        excess = score + (row_base + (logs[:, 0:1] + logs[:, 1:2] + logs[:, 2:3]))
        fitted = (0.1 + 0.25 * jnp.sqrt(count)) * (excess - jnp.log(jnp.maximum(count, 1.0)))
        slope = jnp.where(count > 0.0, fitted, 0.5 + 0.5 * jnp.tanh(0.5 * excess)).astype(BF16)
        slope_ref[b : b + block, :] = slope
        grad = jnp.dot(slope, row_half, preferred_element_type=F32)
        grad_ref[b : b + block, :] = grad.astype(grad_ref.dtype)


def slopes(half, order, col_half, near, row_half, row_marg, count, logs, words, kind):
    cells, rows = col_half.shape[0], row_half.shape[0]
    vmem = pl.BlockSpec(memory_space=pltpu.VMEM)
    return pl.pallas_call(
        functools.partial(slope_kernel, words),
        in_specs=[pl.BlockSpec(memory_space=pltpu.SMEM), pl.BlockSpec(memory_space=pl.ANY)] + [vmem] * 6,
        out_shape=[jax.ShapeDtypeStruct((cells, rows), BF16), jax.ShapeDtypeStruct((cells, WIDE), kind)],
        compiler_params=PARAMS,
    )(half, order, col_half, near, row_half, row_marg, count, logs)


def row_grad_kernel(place_ref, own_ref, other_ref, keep_slope_ref, give_slope_ref, keep_ref, give_ref, total):
    x, zl = place_ref[0], place_ref[1]
    size = keep_ref.shape[1]
    contract = (((0,), (0,)), ((), ()))
    grad = lax.dot_general(own_ref[...], keep_slope_ref[...], contract, preferred_element_type=F32)
    grad += lax.dot_general(other_ref[...], give_slope_ref[...], contract, preferred_element_type=F32)
    total[...] = grad.T
    for i in range(4):
        block = 2 * jnp.bitwise_xor(x, i) + zl
        keep_ref[i] = total[pl.ds(pl.multiple_of(block * size, size), size), :]
        block = jnp.bitwise_xor(block, 1)
        give_ref[i] = total[pl.ds(pl.multiple_of(block * size, size), size), :].astype(BF16)


def row_grads(place, own, other, keep_slope, give_slope, size):
    rows = keep_slope.shape[1]
    vmem = pl.BlockSpec(memory_space=pltpu.VMEM)
    return pl.pallas_call(
        row_grad_kernel,
        in_specs=[pl.BlockSpec(memory_space=pltpu.SMEM)] + [vmem] * 4,
        out_shape=[
            jax.ShapeDtypeStruct((4, size, WIDE), F32),
            jax.ShapeDtypeStruct((4, size, WIDE), BF16),
        ],
        scratch_shapes=[pltpu.VMEM((rows, WIDE), F32)],
        compiler_params=PARAMS,
    )(place, own, other, keep_slope, give_slope)


def after(value, *others):
    anywhere = pl.BlockSpec(memory_space=pl.ANY)
    return pl.pallas_call(
        lambda *refs: None,
        in_specs=[anywhere] * (1 + len(others)),
        out_specs=anywhere,
        out_shape=jax.ShapeDtypeStruct(value.shape, value.dtype),
        input_output_aliases={0: 0},
        compiler_params=pltpu.CompilerParams(vmem_limit_bytes=1024 * 1024),
    )(value, *others)


def adagrad(embedding, accumulator, gradient):
    new_acc = accumulator + gradient * gradient
    return (embedding - gradient / jnp.sqrt(new_acc), new_acc)


def exchange(blocks):
    return lax.all_to_all(blocks, CHIP_AXES, 0, 0, tiled=True)


def flip(block, axis, mask):
    return lax.ppermute(block, axis, [(i, i ^ mask) for i in range(lax.axis_size(axis))])


def body(counts, row_marg, col_marg, row_emb, col_emb, row_acc, col_acc):
    n_chip = lax.axis_size(CHIP_AXES)
    rows, cols = counts.shape
    depth, words = col_emb.shape
    size = row_emb.shape[1]
    core = lax.axis_index("core")
    place = jnp.stack([lax.axis_index("x"), lax.axis_index("zl"), core]).astype(jnp.int32)

    row_line, col_line = row_marg.reshape(1, rows), col_marg.reshape(1, cols)
    own, col_own, total = prepare_own(row_marg.reshape(rows // 128, 128), row_emb.T, col_emb.T)
    beside = flip(own, "zl", 1)
    send = prepare_send(total, flip(total, "core", 1), col_own, n_chip, words)
    mine = exchange(after(send, beside))
    both = jnp.stack([own, beside])
    row_half = assemble_rows(place, [both] + [flip(both, "x", k) for k in (1, 2, 3)]).reshape(rows, WIDE)
    count, logs = cell_tables(counts, col_line, n_chip, words)
    shape = (n_chip, GROUP, WIDE)
    mine = after(mine, row_half, count)
    far = flip(mine, "core", 1).reshape(n_chip * GROUP, WIDE)
    near = mine.reshape(n_chip * GROUP, WIDE)

    tables = (near, row_half, row_line, count, logs, words)
    keep_slope, keep = slopes(core.reshape(1), near, near, *tables, F32)
    give_slope, give = slopes((1 - core).reshape(1), keep_slope, far, *tables, BF16)
    other = flip(give.reshape(shape), "core", 1)
    pair = (keep.reshape(shape) + other.astype(F32)).astype(BF16)
    col_share = jnp.sum(exchange(pair)[:, :words, :depth].astype(F32), axis=0)

    row_keep, row_give = row_grads(place, near, far, keep_slope, give_slope, size)
    row_keep = row_keep + flip(row_give, "zl", 1).astype(F32)
    row_share = row_keep[0]
    for k in (1, 2, 3):
        row_share = row_share + flip(row_keep[k].astype(BF16), "x", k).astype(F32)
    row_share = row_share[:, :depth]

    new_row_emb, new_row_acc = adagrad(row_emb.T, row_acc.T, row_share)
    new_col_emb, new_col_acc = adagrad(col_emb.T, col_acc.T, col_share)
    return (new_row_emb.T, new_col_emb.T, new_row_acc.T, new_col_acc.T)


def solution(mesh):
    fine = Mesh(mesh.devices.reshape(4, 8, 2, 4, 2), ("zh", "y", "core", "x", "zl"))
    return jax.shard_map(
        body,
        mesh=fine,
        in_specs=(
            P(ROW_AXES, COL_AXES),
            P(ROW_AXES),
            P(COL_AXES),
            P(None, ROW_AXES + COL_AXES),
            P(None, COL_AXES + ROW_AXES),
            P(None, ROW_AXES + COL_AXES),
            P(None, COL_AXES + ROW_AXES),
        ),
        out_specs=(
            P(None, ROW_AXES + COL_AXES),
            P(None, COL_AXES + ROW_AXES),
            P(None, ROW_AXES + COL_AXES),
            P(None, COL_AXES + ROW_AXES),
        ),
        check_vma=False,
    )
```

```python
import functools

import jax
import jax.numpy as jnp
from jax import lax
from jax.experimental import pallas as pl
from jax.experimental.pallas import tpu as pltpu
from jax.sharding import Mesh, PartitionSpec as P

ROW_AXES = ("zh", "y", "core")
COL_AXES = ("x", "zl")
CHIP_AXES = ("zh", "y")
GROUP = 24
WINDOW = 640
WIDE = 384
F32, BF16 = jnp.float32, jnp.bfloat16
PARAMS = pltpu.CompilerParams(vmem_limit_bytes=20 * 1024 * 1024)


def widen(value):
    rows, depth = value.shape
    return jnp.concatenate([value, jnp.zeros((rows, WIDE - depth), value.dtype)], axis=1)


def own_kernel(marg_hbm, row_hbm, col_hbm, own_ref, col_ref, total_ref, marg, rows, cols, sems):
    load_marg = pltpu.make_async_copy(marg_hbm, marg, sems.at[0])
    load_row = pltpu.make_async_copy(row_hbm, rows, sems.at[1])
    load_col = pltpu.make_async_copy(col_hbm, cols, sems.at[2])
    load_marg.start()
    load_row.start()
    load_col.start()
    load_marg.wait()
    total = jnp.sum(marg[...], axis=(0, 1), keepdims=True).astype(F32)
    total_ref[...] = jnp.broadcast_to(total, total_ref.shape)
    load_row.wait()
    own_ref[...] = widen(rows[...]).astype(BF16)
    load_col.wait()
    rest = GROUP - cols.shape[0]
    col_ref[...] = jnp.concatenate([widen(cols[...]), jnp.zeros((rest, WIDE), F32)], axis=0)


def prepare_own(row_marg, row_t, col_t):
    return pl.pallas_call(
        own_kernel,
        in_specs=[pl.BlockSpec(memory_space=pltpu.HBM)] * 3,
        out_shape=(
            jax.ShapeDtypeStruct((row_t.shape[0], WIDE), BF16),
            jax.ShapeDtypeStruct((GROUP, WIDE), F32),
            jax.ShapeDtypeStruct((8, 128), F32),
        ),
        scratch_shapes=[
            pltpu.VMEM(row_marg.shape, jnp.int32),
            pltpu.VMEM(row_t.shape, F32),
            pltpu.VMEM(col_t.shape, F32),
            pltpu.SemaphoreType.DMA((3,)),
        ],
        compiler_params=PARAMS,
    )(*[pltpu.with_memory_space_constraint(a, pltpu.HBM) for a in (row_marg, row_t, col_t)])


def send_kernel(words, total_ref, rest_ref, col_ref, send_ref):
    total = total_ref[0:1, 0:1] + rest_ref[0:1, 0:1]
    high = total.astype(BF16).astype(F32)
    middle = (total - high).astype(BF16).astype(F32)
    low = total - high - middle
    line = lax.broadcasted_iota(jnp.int32, (GROUP, WIDE), 0)
    lane = lax.broadcasted_iota(jnp.int32, (GROUP, WIDE), 1)
    parts = jnp.where(lane == 0, high, jnp.where(lane == 1, middle, jnp.where(lane == 2, low, 0.0)))
    value = jnp.where(line == words, parts, col_ref[...]).astype(BF16)
    for i in range(send_ref.shape[0]):
        send_ref[i] = value


def prepare_send(total, rest, col_own, n_chip, words):
    return pl.pallas_call(
        functools.partial(send_kernel, words),
        out_shape=jax.ShapeDtypeStruct((n_chip, GROUP, WIDE), BF16),
        compiler_params=PARAMS,
    )(total, rest, col_own)


def group_of(number):
    return jnp.right_shift(number * 2731, 16)


def cells_kernel(words, marg_ref, counts_hbm, count_ref, logs_ref, counts, pick, sems):
    rows, cols = counts_hbm.shape
    cells = count_ref.shape[0] // 2
    half = cells // 2
    block = 256
    loads = [
        pltpu.make_async_copy(counts_hbm.at[r : r + block], counts.at[r : r + block], sems.at[r // block])
        for r in range(0, rows, block)
    ]
    for load in loads:
        load.start()
    log = jnp.log(marg_ref[...].astype(F32))
    high = log.astype(BF16).astype(F32)
    middle = (log - high).astype(BF16).astype(F32)
    low = log - high - middle
    line = lax.broadcasted_iota(jnp.int32, (128, cols), 0)
    stack = jnp.where(line == 0, high, jnp.where(line == 1, middle, jnp.where(line == 2, low, 1.0)))
    stack = stack.astype(BF16)
    lane = lax.broadcasted_iota(jnp.int32, (half, WINDOW), 1)
    place = lax.broadcasted_iota(jnp.int32, (half, 1), 0)
    group = group_of(place)
    word = place - GROUP * group
    column = lax.broadcasted_iota(jnp.int32, (half, 128), 1)
    for m in range(2):
        window = slice(m * (cols - WINDOW), m * (cols - WINDOW) + WINDOW)
        for c in range(2):
            target = (2 * group + (m * half // GROUP * 2 + c)) * words + word - window.start
            target = jnp.where(word < words, target, -1)
            at = slice(c * cells + m * half, c * cells + (m + 1) * half)
            hit = jnp.where(lane == target, 1.0, 0.0).astype(BF16)
            pick[at, :] = hit
            found = lax.dot_general(hit, stack[:, window], (((1,), (1,)), ((), ())), preferred_element_type=F32)
            found = jnp.where(column < 3, found, 0.0)
            found = jnp.where((column == 0) & (word >= words), -1e30, found)
            logs_ref[at, :] = found.astype(BF16)
    for r in range(0, rows, block):
        loads[r // block].wait()
        for m in range(2):
            window = slice(m * (cols - WINDOW), m * (cols - WINDOW) + WINDOW)
            part = counts[r : r + block, window].astype(F32).astype(BF16)
            for c in range(2):
                at = slice(c * cells + m * half, c * cells + (m + 1) * half)
                count = lax.dot_general(pick[at, :], part, (((1,), (1,)), ((), ())), preferred_element_type=F32)
                count_ref[at, r : r + block] = count.astype(jnp.int32).astype(jnp.int8)


def cell_tables(counts, col_marg, n_chip, words):
    rows, cols = counts.shape
    cells = n_chip * GROUP
    return pl.pallas_call(
        functools.partial(cells_kernel, words),
        in_specs=[pl.BlockSpec(memory_space=pltpu.VMEM), pl.BlockSpec(memory_space=pltpu.HBM)],
        out_shape=(jax.ShapeDtypeStruct((2 * cells, rows), jnp.int8), jax.ShapeDtypeStruct((2 * cells, 128), BF16)),
        scratch_shapes=[
            pltpu.VMEM((rows, cols), jnp.int32),
            pltpu.VMEM((2 * cells, WINDOW), BF16),
            pltpu.SemaphoreType.DMA((rows // 256,)),
        ],
        compiler_params=PARAMS,
    )(col_marg, pltpu.with_memory_space_constraint(counts, pltpu.HBM))


def rows_kernel(place_ref, *refs):
    x, zl = place_ref[0], place_ref[1]
    for k in range(4):
        for b in range(2):
            block = 2 * jnp.bitwise_xor(x, k) + jnp.bitwise_xor(zl, b)
            refs[4][block] = refs[k][b]


def assemble_rows(place, pairs):
    size, depth = pairs[0].shape[1:]
    vmem = pl.BlockSpec(memory_space=pltpu.VMEM)
    return pl.pallas_call(
        rows_kernel,
        in_specs=[pl.BlockSpec(memory_space=pltpu.SMEM)] + [vmem] * 4,
        out_shape=jax.ShapeDtypeStruct((8, size, depth), BF16),
        compiler_params=PARAMS,
    )(place, *pairs)


def slope_kernel(words, half_ref, order_ref, col_ref, near_ref, row_ref, marg_ref, count_ref, logs_ref, slope_ref, grad_ref):
    cells, rows = slope_ref.shape
    place = lax.broadcasted_iota(jnp.int32, (16, cells), 1)
    pick = jnp.where(place - GROUP * group_of(place) == words, 1.0, 0.0).astype(BF16)
    parts = jnp.dot(pick, near_ref[...], preferred_element_type=F32)
    log_total = jnp.log(jnp.sum(parts[0:1, 0:128], axis=1, keepdims=True))
    row_base = jnp.log(marg_ref[...].astype(F32)) - log_total
    first = half_ref[0] * cells
    row_half = row_ref[...]
    block = 256
    for b in range(0, cells, block):
        at = pl.ds(pl.multiple_of(first + b, block), block)
        score = lax.dot_general(
            col_ref[b : b + block, :], row_half, (((1,), (1,)), ((), ())), preferred_element_type=F32
        )
        count = count_ref[at, :].astype(jnp.int32).astype(F32)
        logs = logs_ref[at, :].astype(F32)
        excess = score + (row_base + (logs[:, 0:1] + logs[:, 1:2] + logs[:, 2:3]))
        least = jnp.maximum(count, 1.0)
        fitted = (0.1 + 0.25 * (least * lax.rsqrt(least))) * (excess - jnp.log(least))
        slope = jnp.where(count > 0.0, fitted, 0.5 + 0.5 * jnp.tanh(0.5 * excess)).astype(BF16)
        slope_ref[b : b + block, :] = slope
        grad = jnp.dot(slope, row_half, preferred_element_type=F32)
        grad_ref[b : b + block, :] = grad.astype(grad_ref.dtype)


def slopes(half, order, col_half, near, row_half, row_marg, count, logs, words, kind):
    cells, rows = col_half.shape[0], row_half.shape[0]
    vmem = pl.BlockSpec(memory_space=pltpu.VMEM)
    return pl.pallas_call(
        functools.partial(slope_kernel, words),
        in_specs=[pl.BlockSpec(memory_space=pltpu.SMEM), pl.BlockSpec(memory_space=pl.ANY)] + [vmem] * 6,
        out_shape=[jax.ShapeDtypeStruct((cells, rows), BF16), jax.ShapeDtypeStruct((cells, WIDE), kind)],
        compiler_params=PARAMS,
    )(half, order, col_half, near, row_half, row_marg, count, logs)


def row_grad_kernel(place_ref, own_ref, other_ref, keep_slope_ref, give_slope_ref, keep_ref, give_ref, total):
    x, zl = place_ref[0], place_ref[1]
    size = keep_ref.shape[1]
    contract = (((0,), (0,)), ((), ()))
    used = 304
    grad = lax.dot_general(own_ref[:, :used], keep_slope_ref[...], contract, preferred_element_type=F32)
    grad += lax.dot_general(other_ref[:, :used], give_slope_ref[...], contract, preferred_element_type=F32)
    total[...] = widen(grad.T)
    for i in range(4):
        block = 2 * jnp.bitwise_xor(x, i) + zl
        keep_ref[i] = total[pl.ds(pl.multiple_of(block * size, size), size), :]
        block = jnp.bitwise_xor(block, 1)
        give_ref[i] = total[pl.ds(pl.multiple_of(block * size, size), size), :].astype(BF16)


def row_grads(place, own, other, keep_slope, give_slope, size):
    rows = keep_slope.shape[1]
    vmem = pl.BlockSpec(memory_space=pltpu.VMEM)
    return pl.pallas_call(
        row_grad_kernel,
        in_specs=[pl.BlockSpec(memory_space=pltpu.SMEM)] + [vmem] * 4,
        out_shape=[
            jax.ShapeDtypeStruct((4, size, WIDE), F32),
            jax.ShapeDtypeStruct((4, size, WIDE), BF16),
        ],
        scratch_shapes=[pltpu.VMEM((rows, WIDE), F32)],
        compiler_params=PARAMS,
    )(place, own, other, keep_slope, give_slope)


def after(value, *others):
    anywhere = pl.BlockSpec(memory_space=pl.ANY)
    return pl.pallas_call(
        lambda *refs: None,
        in_specs=[anywhere] * (1 + len(others)),
        out_specs=anywhere,
        out_shape=jax.ShapeDtypeStruct(value.shape, value.dtype),
        input_output_aliases={0: 0},
        compiler_params=pltpu.CompilerParams(vmem_limit_bytes=1024 * 1024),
    )(value, *others)


def adagrad(embedding, accumulator, gradient):
    new_acc = accumulator + gradient * gradient
    return (embedding - gradient / jnp.sqrt(new_acc), new_acc)


def exchange(blocks):
    return lax.all_to_all(blocks, CHIP_AXES, 0, 0, tiled=True)


def flip(block, axis, mask):
    return lax.ppermute(block, axis, [(i, i ^ mask) for i in range(lax.axis_size(axis))])


def body(counts, row_marg, col_marg, row_emb, col_emb, row_acc, col_acc):
    n_chip = lax.axis_size(CHIP_AXES)
    rows, cols = counts.shape
    depth, words = col_emb.shape
    size = row_emb.shape[1]
    core = lax.axis_index("core")
    place = jnp.stack([lax.axis_index("x"), lax.axis_index("zl"), core]).astype(jnp.int32)

    row_line, col_line = row_marg.reshape(1, rows), col_marg.reshape(1, cols)
    own, col_own, total = prepare_own(row_marg.reshape(rows // 128, 128), row_emb.T, col_emb.T)
    beside = flip(own, "zl", 1)
    send = prepare_send(total, flip(total, "core", 1), col_own, n_chip, words)
    mine = exchange(after(send, beside))
    both = jnp.stack([own, beside])
    row_half = assemble_rows(place, [both] + [flip(both, "x", k) for k in (1, 2, 3)]).reshape(rows, WIDE)
    count, logs = cell_tables(counts, col_line, n_chip, words)
    shape = (n_chip, GROUP, WIDE)
    mine = after(mine, row_half, count)
    far = flip(mine, "core", 1).reshape(n_chip * GROUP, WIDE)
    near = mine.reshape(n_chip * GROUP, WIDE)

    tables = (near, row_half, row_line, count, logs, words)
    keep_slope, keep = slopes(core.reshape(1), near, near, *tables, F32)
    give_slope, give = slopes((1 - core).reshape(1), keep_slope, far, *tables, BF16)
    other = flip(give.reshape(shape), "core", 1)
    pair = (keep.reshape(shape) + other.astype(F32)).astype(BF16)
    col_share = jnp.sum(exchange(pair)[:, :words, :depth].astype(F32), axis=0)

    row_keep, row_give = row_grads(place, near, far, keep_slope, give_slope, size)
    row_keep = row_keep + flip(row_give, "zl", 1).astype(F32)
    row_share = row_keep[0]
    for k in (1, 2, 3):
        row_share = row_share + flip(row_keep[k].astype(BF16), "x", k).astype(F32)
    row_share = row_share[:, :depth]

    new_row_emb, new_row_acc = adagrad(row_emb.T, row_acc.T, row_share)
    new_col_emb, new_col_acc = adagrad(col_emb.T, col_acc.T, col_share)
    return (new_row_emb.T, new_col_emb.T, new_row_acc.T, new_col_acc.T)


def solution(mesh):
    fine = Mesh(mesh.devices.reshape(4, 8, 2, 4, 2), ("zh", "y", "core", "x", "zl"))
    return jax.shard_map(
        body,
        mesh=fine,
        in_specs=(
            P(ROW_AXES, COL_AXES),
            P(ROW_AXES),
            P(COL_AXES),
            P(None, ROW_AXES + COL_AXES),
            P(None, COL_AXES + ROW_AXES),
            P(None, ROW_AXES + COL_AXES),
            P(None, COL_AXES + ROW_AXES),
        ),
        out_specs=(
            P(None, ROW_AXES + COL_AXES),
            P(None, COL_AXES + ROW_AXES),
            P(None, ROW_AXES + COL_AXES),
            P(None, COL_AXES + ROW_AXES),
        ),
        check_vma=False,
    )
```

```python
import functools

import jax
import jax.numpy as jnp
from jax import lax
from jax.experimental import pallas as pl
from jax.experimental.pallas import tpu as pltpu
from jax.sharding import Mesh, PartitionSpec as P

ROW_AXES = ("zh", "y", "core")
COL_AXES = ("x", "zl")
CHIP_AXES = ("zh", "y")
GROUP = 24
WINDOW = 640
WIDE = 384
F32, BF16 = jnp.float32, jnp.bfloat16
PARAMS = pltpu.CompilerParams(vmem_limit_bytes=20 * 1024 * 1024)


def widen(value):
    rows, depth = value.shape
    return jnp.concatenate([value, jnp.zeros((rows, WIDE - depth), value.dtype)], axis=1)


def own_kernel(marg_hbm, row_hbm, col_hbm, own_ref, col_ref, total_ref, marg, rows, cols, sems):
    load_marg = pltpu.make_async_copy(marg_hbm, marg, sems.at[0])
    load_row = pltpu.make_async_copy(row_hbm, rows, sems.at[1])
    load_col = pltpu.make_async_copy(col_hbm, cols, sems.at[2])
    load_marg.start()
    load_row.start()
    load_col.start()
    load_marg.wait()
    total = jnp.sum(marg[...], axis=(0, 1), keepdims=True).astype(F32)
    total_ref[...] = jnp.broadcast_to(total, total_ref.shape)
    load_row.wait()
    own_ref[...] = widen(rows[...]).astype(BF16)
    load_col.wait()
    rest = GROUP - cols.shape[0]
    col_ref[...] = jnp.concatenate([widen(cols[...]), jnp.zeros((rest, WIDE), F32)], axis=0)


def prepare_own(row_marg, row_t, col_t):
    return pl.pallas_call(
        own_kernel,
        in_specs=[pl.BlockSpec(memory_space=pltpu.HBM)] * 3,
        out_shape=(
            jax.ShapeDtypeStruct((row_t.shape[0], WIDE), BF16),
            jax.ShapeDtypeStruct((GROUP, WIDE), F32),
            jax.ShapeDtypeStruct((8, 128), F32),
        ),
        scratch_shapes=[
            pltpu.VMEM(row_marg.shape, jnp.int32),
            pltpu.VMEM(row_t.shape, F32),
            pltpu.VMEM(col_t.shape, F32),
            pltpu.SemaphoreType.DMA((3,)),
        ],
        compiler_params=PARAMS,
    )(*[pltpu.with_memory_space_constraint(a, pltpu.HBM) for a in (row_marg, row_t, col_t)])


def send_kernel(words, totals_ref, col_ref, send_ref):
    total = totals_ref[0, 0:1, 0:1] + totals_ref[1, 0:1, 0:1]
    high = total.astype(BF16).astype(F32)
    middle = (total - high).astype(BF16).astype(F32)
    low = total - high - middle
    line = lax.broadcasted_iota(jnp.int32, (GROUP, WIDE), 0)
    lane = lax.broadcasted_iota(jnp.int32, (GROUP, WIDE), 1)
    parts = jnp.where(lane == 0, high, jnp.where(lane == 1, middle, jnp.where(lane == 2, low, 0.0)))
    value = jnp.where(line == words, parts, col_ref[...]).astype(BF16)
    for i in range(send_ref.shape[0]):
        send_ref[i] = value


def prepare_send(totals, col_own, n_chip, words):
    return pl.pallas_call(
        functools.partial(send_kernel, words),
        out_shape=jax.ShapeDtypeStruct((n_chip, GROUP, WIDE), BF16),
        compiler_params=PARAMS,
    )(totals, col_own)


def group_of(number):
    return jnp.right_shift(number * 2731, 16)


def cells_kernel(words, marg_ref, counts_hbm, count_ref, logs_ref, counts, pick, sems):
    rows, cols = counts_hbm.shape
    cells = count_ref.shape[0] // 2
    half = cells // 2
    block = 256
    loads = [
        pltpu.make_async_copy(counts_hbm.at[r : r + block], counts.at[r : r + block], sems.at[r // block])
        for r in range(0, rows, block)
    ]
    for load in loads:
        load.start()
    log = jnp.log(marg_ref[...].astype(F32))
    high = log.astype(BF16).astype(F32)
    middle = (log - high).astype(BF16).astype(F32)
    low = log - high - middle
    line = lax.broadcasted_iota(jnp.int32, (128, cols), 0)
    stack = jnp.where(line == 0, high, jnp.where(line == 1, middle, jnp.where(line == 2, low, 1.0)))
    stack = stack.astype(BF16)
    lane = lax.broadcasted_iota(jnp.int32, (half, WINDOW), 1)
    place = lax.broadcasted_iota(jnp.int32, (half, 1), 0)
    group = group_of(place)
    word = place - GROUP * group
    column = lax.broadcasted_iota(jnp.int32, (half, 128), 1)
    for m in range(2):
        window = slice(m * (cols - WINDOW), m * (cols - WINDOW) + WINDOW)
        for c in range(2):
            target = (2 * group + (m * half // GROUP * 2 + c)) * words + word - window.start
            target = jnp.where(word < words, target, -1)
            at = slice(c * cells + m * half, c * cells + (m + 1) * half)
            hit = jnp.where(lane == target, 1.0, 0.0).astype(BF16)
            pick[at, :] = hit
            found = lax.dot_general(hit, stack[:, window], (((1,), (1,)), ((), ())), preferred_element_type=F32)
            found = jnp.where(column < 3, found, 0.0)
            found = jnp.where((column == 0) & (word >= words), -1e30, found)
            logs_ref[at, :] = found.astype(BF16)
    for r in range(0, rows, block):
        loads[r // block].wait()
        for m in range(2):
            window = slice(m * (cols - WINDOW), m * (cols - WINDOW) + WINDOW)
            part = counts[r : r + block, window].astype(F32).astype(BF16)
            for c in range(2):
                at = slice(c * cells + m * half, c * cells + (m + 1) * half)
                count = lax.dot_general(pick[at, :], part, (((1,), (1,)), ((), ())), preferred_element_type=F32)
                count_ref[at, r : r + block] = count.astype(jnp.int32).astype(jnp.int8)


def cell_tables(counts, col_marg, n_chip, words):
    rows, cols = counts.shape
    cells = n_chip * GROUP
    return pl.pallas_call(
        functools.partial(cells_kernel, words),
        in_specs=[pl.BlockSpec(memory_space=pltpu.VMEM), pl.BlockSpec(memory_space=pltpu.HBM)],
        out_shape=(jax.ShapeDtypeStruct((2 * cells, rows), jnp.int8), jax.ShapeDtypeStruct((2 * cells, 128), BF16)),
        scratch_shapes=[
            pltpu.VMEM((rows, cols), jnp.int32),
            pltpu.VMEM((2 * cells, WINDOW), BF16),
            pltpu.SemaphoreType.DMA((rows // 256,)),
        ],
        compiler_params=PARAMS,
    )(col_marg, pltpu.with_memory_space_constraint(counts, pltpu.HBM))


def rows_kernel(place_ref, *refs):
    x, zl = place_ref[0], place_ref[1]
    for k in range(4):
        for b in range(2):
            block = 2 * jnp.bitwise_xor(x, k) + jnp.bitwise_xor(zl, b)
            refs[4][block] = refs[k][b]


def assemble_rows(place, pairs):
    size, depth = pairs[0].shape[1:]
    vmem = pl.BlockSpec(memory_space=pltpu.VMEM)
    return pl.pallas_call(
        rows_kernel,
        in_specs=[pl.BlockSpec(memory_space=pltpu.SMEM)] + [vmem] * 4,
        out_shape=jax.ShapeDtypeStruct((8, size, depth), BF16),
        compiler_params=PARAMS,
    )(place, *pairs)


def slope_kernel(words, half_ref, order_ref, col_ref, near_ref, row_ref, marg_ref, count_ref, logs_ref, slope_ref, grad_ref):
    cells, rows = slope_ref.shape
    place = lax.broadcasted_iota(jnp.int32, (16, cells), 1)
    pick = jnp.where(place - GROUP * group_of(place) == words, 1.0, 0.0).astype(BF16)
    parts = jnp.dot(pick, near_ref[...], preferred_element_type=F32)
    log_total = jnp.log(jnp.sum(parts[0:1, 0:128], axis=1, keepdims=True))
    row_base = jnp.log(marg_ref[...].astype(F32)) - log_total
    first = half_ref[0] * cells
    row_half = row_ref[...]
    block = 256
    for b in range(0, cells, block):
        at = pl.ds(pl.multiple_of(first + b, block), block)
        score = lax.dot_general(
            col_ref[b : b + block, :], row_half, (((1,), (1,)), ((), ())), preferred_element_type=F32
        )
        count = count_ref[at, :].astype(jnp.int32).astype(F32)
        logs = logs_ref[at, :].astype(F32)
        excess = score + (row_base + (logs[:, 0:1] + logs[:, 1:2] + logs[:, 2:3]))
        least = jnp.maximum(count, 1.0)
        fitted = (0.1 + 0.25 * (least * lax.rsqrt(least))) * (excess - jnp.log(least))
        slope = jnp.where(count > 0.0, fitted, 0.5 + 0.5 * jnp.tanh(0.5 * excess)).astype(BF16)
        slope_ref[b : b + block, :] = slope
        grad = jnp.dot(slope, row_half, preferred_element_type=F32)
        grad_ref[b : b + block, :] = grad.astype(grad_ref.dtype)


def slopes(half, order, col_half, near, row_half, row_marg, count, logs, words, kind):
    cells, rows = col_half.shape[0], row_half.shape[0]
    vmem = pl.BlockSpec(memory_space=pltpu.VMEM)
    return pl.pallas_call(
        functools.partial(slope_kernel, words),
        in_specs=[pl.BlockSpec(memory_space=pltpu.SMEM), pl.BlockSpec(memory_space=pl.ANY)] + [vmem] * 6,
        out_shape=[jax.ShapeDtypeStruct((cells, rows), BF16), jax.ShapeDtypeStruct((cells, WIDE), kind)],
        compiler_params=PARAMS,
    )(half, order, col_half, near, row_half, row_marg, count, logs)


def row_grad_kernel(place_ref, own_ref, other_ref, keep_slope_ref, give_slope_ref, keep_ref, give_ref, total):
    x, zl = place_ref[0], place_ref[1]
    size = keep_ref.shape[1]
    contract = (((0,), (0,)), ((), ()))
    used = 304
    grad = lax.dot_general(own_ref[:, :used], keep_slope_ref[...], contract, preferred_element_type=F32)
    grad += lax.dot_general(other_ref[:, :used], give_slope_ref[...], contract, preferred_element_type=F32)
    total[...] = widen(grad.T)
    for i in range(4):
        block = 2 * jnp.bitwise_xor(x, i) + zl
        keep_ref[i] = total[pl.ds(pl.multiple_of(block * size, size), size), :]
        block = jnp.bitwise_xor(block, 1)
        give_ref[i] = total[pl.ds(pl.multiple_of(block * size, size), size), :].astype(BF16)


def row_grads(place, own, other, keep_slope, give_slope, size):
    rows = keep_slope.shape[1]
    vmem = pl.BlockSpec(memory_space=pltpu.VMEM)
    return pl.pallas_call(
        row_grad_kernel,
        in_specs=[pl.BlockSpec(memory_space=pltpu.SMEM)] + [vmem] * 4,
        out_shape=[
            jax.ShapeDtypeStruct((4, size, WIDE), F32),
            jax.ShapeDtypeStruct((4, size, WIDE), BF16),
        ],
        scratch_shapes=[pltpu.VMEM((rows, WIDE), F32)],
        compiler_params=PARAMS,
    )(place, own, other, keep_slope, give_slope)


def after(value, *others):
    anywhere = pl.BlockSpec(memory_space=pl.ANY)
    return pl.pallas_call(
        lambda *refs: None,
        in_specs=[anywhere] * (1 + len(others)),
        out_specs=anywhere,
        out_shape=jax.ShapeDtypeStruct(value.shape, value.dtype),
        input_output_aliases={0: 0},
        compiler_params=pltpu.CompilerParams(vmem_limit_bytes=1024 * 1024),
    )(value, *others)


def adagrad(embedding, accumulator, gradient):
    new_acc = accumulator + gradient * gradient
    return (embedding - gradient / jnp.sqrt(new_acc), new_acc)


def exchange(blocks):
    return lax.all_to_all(blocks, CHIP_AXES, 0, 0, tiled=True)


def flip(block, axis, mask):
    return lax.ppermute(block, axis, [(i, i ^ mask) for i in range(lax.axis_size(axis))])


def body(counts, row_marg, col_marg, row_emb, col_emb, row_acc, col_acc):
    n_chip = lax.axis_size(CHIP_AXES)
    rows, cols = counts.shape
    depth, words = col_emb.shape
    size = row_emb.shape[1]
    core = lax.axis_index("core")
    place = jnp.stack([lax.axis_index("x"), lax.axis_index("zl"), core]).astype(jnp.int32)

    row_line, col_line = row_marg.reshape(1, rows), col_marg.reshape(1, cols)
    own, col_own, total = prepare_own(row_marg.reshape(rows // 128, 128), row_emb.T, col_emb.T)
    beside = flip(own, "zl", 1)
    send = prepare_send(lax.all_gather(total, "core", axis=0), col_own, n_chip, words)
    mine = exchange(after(send, beside))
    both = jnp.stack([own, beside])
    row_half = assemble_rows(place, [both] + [flip(both, "x", k) for k in (1, 2, 3)]).reshape(rows, WIDE)
    count, logs = cell_tables(counts, col_line, n_chip, words)
    shape = (n_chip, GROUP, WIDE)
    mine = after(mine, row_half, count)
    far = flip(mine, "core", 1).reshape(n_chip * GROUP, WIDE)
    near = mine.reshape(n_chip * GROUP, WIDE)

    tables = (near, row_half, row_line, count, logs, words)
    keep_slope, keep = slopes(core.reshape(1), near, near, *tables, F32)
    give_slope, give = slopes((1 - core).reshape(1), keep_slope, far, *tables, BF16)
    other = flip(give.reshape(shape), "core", 1)
    pair = (keep.reshape(shape) + other.astype(F32)).astype(BF16)
    col_share = jnp.sum(exchange(pair)[:, :words, :depth].astype(F32), axis=0)

    row_keep, row_give = row_grads(place, near, far, keep_slope, give_slope, size)
    row_keep = row_keep + flip(row_give, "zl", 1).astype(F32)
    row_share = row_keep[0]
    for k in (1, 2, 3):
        row_share = row_share + flip(row_keep[k].astype(BF16), "x", k).astype(F32)
    row_share = row_share[:, :depth]

    new_row_emb, new_row_acc = adagrad(row_emb.T, row_acc.T, row_share)
    new_col_emb, new_col_acc = adagrad(col_emb.T, col_acc.T, col_share)
    return (new_row_emb.T, new_col_emb.T, new_row_acc.T, new_col_acc.T)


def solution(mesh):
    fine = Mesh(mesh.devices.reshape(4, 8, 2, 4, 2), ("zh", "y", "core", "x", "zl"))
    return jax.shard_map(
        body,
        mesh=fine,
        in_specs=(
            P(ROW_AXES, COL_AXES),
            P(ROW_AXES),
            P(COL_AXES),
            P(None, ROW_AXES + COL_AXES),
            P(None, COL_AXES + ROW_AXES),
            P(None, ROW_AXES + COL_AXES),
            P(None, COL_AXES + ROW_AXES),
        ),
        out_specs=(
            P(None, ROW_AXES + COL_AXES),
            P(None, COL_AXES + ROW_AXES),
            P(None, ROW_AXES + COL_AXES),
            P(None, COL_AXES + ROW_AXES),
        ),
        check_vma=False,
    )
```
